32 devices in a mesh: dp: 4 (over y, core), context: 8 (over z, x).
Axes of the slice: x: 2, y: 2, z: 4, core: 2. Of those that a mesh axis runs over, the one named last changes fastest.
Arguments:
- query_in: bfloat16 [4, 1024, 8192], P('dp', 'context'), may hold values from -6 to 6
- key_in: bfloat16 [4, 1024, 8192], P('dp', 'context'), may hold values from -6 to 6
- value_in: bfloat16 [4, 1024, 8192], P('dp', 'context'), may hold values from -6 to 6
- grad_out: bfloat16 [4, 1024, 8192], P('dp', 'context'), may hold values from -6 to 6
- med_filter: float32 [8192, 128], P('context', 'dp'), may hold values from -0.5 to 0.5
- short_filter: float32 [3, 8192, 7], P(None, 'context'), may hold values from -2 to 2
Outputs:
- mixed: bfloat16 [4, 1024, 8192], P('dp', 'context')
- grad_q: bfloat16 [4, 1024, 8192], P('dp', 'context')
- grad_k: bfloat16 [4, 1024, 8192], P('dp', 'context')
- grad_v: bfloat16 [4, 1024, 8192], P('dp', 'context')
- grad_med: float32 [8192, 128], P('context', 'dp')
- grad_short: float32 [3, 8192, 7], P(None, 'context')
The draws below stay inside these ranges and needn't reach their ends.
All inputs are finite; a program needn't handle non-finite values.
Results may differ from the reference program's by a relative error of at most 0.0058.
Values may be sent and summed in bfloat16 or wider, within the bound.
A program may use at most 384 MiB of HBM per device.

```python
import jax
import jax.numpy as jnp
from jax import lax

D = 8192
MED = 128
SHORT = 7
LEN = 1024
SEQS = 4
N_CONTEXT = 8


def steps_of(stream_key, shape, cuts, least, top_value):
    def one(position, shards_of):
        steps = jax.random.uniform(jax.random.fold_in(jax.random.fold_in(stream_key, 6), position), (shards_of,), jnp.float32, least / len(cuts), top_value / len(cuts))
        return jnp.repeat(jnp.exp(steps), shape[position] // shards_of).reshape((-1,) + (1,) * (len(shape) - position - 1))

    factor_of = one(*cuts[0])
    for cut in cuts[1:]:
        factor_of = factor_of * one(*cut)
    return factor_of


def normal_values(rng, dims, deviation, reach, pieces=(), held_as=jnp.bfloat16):
    values = deviation * jax.random.normal(rng, dims, jnp.float32)
    if pieces:
        values = values * steps_of(rng, dims, pieces, -0.22, 0.18)
    return jnp.clip(values, -reach, reach).astype(held_as)


def setup_inputs(seed: int = 0) -> dict:
    splits = jax.random.split(jax.random.key(seed), 7)
    return {
        "query_in": normal_values(splits[0], (SEQS, LEN, D), 1.0, 6.0, ((0, 4), (1, 8))),
        "key_in": normal_values(splits[1], (SEQS, LEN, D), 1.0, 6.0, ((0, 4), (1, 8))),
        "value_in": normal_values(splits[2], (SEQS, LEN, D), 1.0, 6.0, ((0, 4), (1, 8))),
        "grad_out": normal_values(splits[3], (SEQS, LEN, D), 1.0, 6.0, ((0, 4), (1, 8))),
        "med_filter": normal_values(splits[4], (D, MED), MED ** -0.5, 0.5, ((0, 8), (1, 4)), jnp.float32),
        "short_filter": normal_values(splits[5], (3, D, SHORT), SHORT ** -0.5, 2.0, ((1, 8),), jnp.float32),
    }


def short_forward(rows, before, taps):
    width = taps.shape[1]
    count = rows.shape[0]
    padded = jnp.concatenate([before, rows], axis=0).astype(jnp.float32)
    total = jnp.zeros(rows.shape, jnp.float32)
    for offset in range(width):
        start = width - 1 - offset
        total = total + taps[:, offset] * padded[start:start + count]
    return total


def short_backward(grads, after, taps):
    width = taps.shape[1]
    count = grads.shape[0]
    padded = jnp.concatenate([grads, after], axis=0)
    total = jnp.zeros(grads.shape, jnp.float32)
    for offset in range(width):
        total = total + taps[:, offset] * padded[offset:offset + count]
    return total


def short_weight(grads, rows, before):
    width = before.shape[0] + 1
    count = rows.shape[0]
    padded = jnp.concatenate([before, rows], axis=0).astype(jnp.float32)
    columns = []
    for offset in range(width):
        start = width - 1 - offset
        columns.append(jnp.sum(grads * padded[start:start + count], axis=0))
    return jnp.stack(columns, axis=1)


def toeplitz(taps):
    size = taps.shape[1]
    index = lax.broadcasted_iota(jnp.int32, (size, 2 * size), 0) + size - lax.broadcasted_iota(jnp.int32, (size, 2 * size), 1)
    valid = (index >= 0) & (index < size)
    picked = taps[:, jnp.clip(index, 0, size - 1)]
    return jnp.where(valid[None], picked, jnp.zeros((), taps.dtype))


def windows(rows, before):
    size = before.shape[0] + 1
    first = jnp.concatenate([jnp.zeros((1, rows.shape[1]), rows.dtype), before], axis=0)
    blocks = rows.reshape(rows.shape[0] // size, size, rows.shape[1])
    earlier = jnp.concatenate([first[None], blocks[:-1]], axis=0)
    return jnp.concatenate([earlier, blocks], axis=1)


def medium_conv(rows, before, toep):
    frames = windows(rows, before).astype(jnp.float32)
    out = jnp.einsum("brc,csr->bsc", frames, toep.astype(jnp.float32))
    return out.reshape(rows.shape)


def medium_weight(grads, rows, before):
    size = before.shape[0] + 1
    frames = windows(rows, before).astype(jnp.float32)
    blocks = grads.reshape(-1, size, grads.shape[1]).astype(jnp.float32)
    outer = jnp.einsum("bsc,brc->csr", blocks, frames)
    chans = outer.shape[0]
    padded = jnp.pad(outer, ((0, 0), (0, 0), (0, 1)))
    flat = padded.reshape(chans, size * (2 * size + 1))
    flat = jnp.pad(flat, ((0, 0), (0, size)))
    sheared = flat.reshape(chans, size, 2 * size + 2)
    return jnp.flip(jnp.sum(sheared[:, :, 1:size + 1], axis=1), axis=1)


def one_sequence(query, keys, values, cotangent, toep, shorts):
    chans = query.shape[1]
    rim_short = jnp.zeros((shorts.shape[2] - 1, chans), jnp.bfloat16)
    rim_med = jnp.zeros((toep.shape[1] - 1, chans), jnp.bfloat16)
    after_short = jnp.zeros((shorts.shape[2] - 1, chans), jnp.float32)
    q_short = short_forward(query, rim_short, shorts[0])
    k_short = short_forward(keys, rim_short, shorts[1])
    v_short = short_forward(values, rim_short, shorts[2])
    product = (k_short * v_short).astype(jnp.bfloat16)
    conv_out = medium_conv(product, rim_med, toep)
    mixed = (q_short * conv_out).astype(jnp.bfloat16)
    grad_f = cotangent.astype(jnp.float32)
    grad_z = (grad_f * q_short).astype(jnp.bfloat16)
    grad_qs = grad_f * conv_out
    grad_u = jnp.flip(medium_conv(jnp.flip(grad_z, 0), rim_med, toep), 0)
    grad_ks = grad_u * v_short
    grad_vs = grad_u * k_short
    grad_q = short_backward(grad_qs, after_short, shorts[0]).astype(jnp.bfloat16)
    grad_k = short_backward(grad_ks, after_short, shorts[1]).astype(jnp.bfloat16)
    grad_v = short_backward(grad_vs, after_short, shorts[2]).astype(jnp.bfloat16)
    grad_med = medium_weight(grad_z, product, rim_med)
    grad_short = jnp.stack([short_weight(grad_qs, query, rim_short), short_weight(grad_ks, keys, rim_short), short_weight(grad_vs, values, rim_short)], axis=0)
    return mixed, grad_q, grad_k, grad_v, grad_med, grad_short


def reference(query_in, key_in, value_in, grad_out, med_filter, short_filter):
    seqs, length, width = query_in.shape
    count = N_CONTEXT
    group = width // count

    def split(x):
        return x.reshape(seqs, length, count, group).transpose(2, 0, 1, 3)

    taps = med_filter.astype(jnp.bfloat16).reshape(count, group, -1)
    shorts = short_filter.reshape(3, count, group, -1).transpose(1, 0, 2, 3)

    def block(items):
        query, keys, values, cotangent, htaps, stap = items
        toep = toeplitz(htaps)
        outs = jax.vmap(lambda a, b, c, d: one_sequence(a, b, c, d, toep, stap))(query, keys, values, cotangent)
        return outs[0], outs[1], outs[2], outs[3], jnp.sum(outs[4], axis=0), jnp.sum(outs[5], axis=0)

    result = lax.map(block, (split(query_in), split(key_in), split(value_in), split(grad_out), taps, shorts))

    def merge(x):
        return x.transpose(1, 2, 0, 3).reshape(seqs, length, width)

    grad_med = result[4].reshape(width, -1)
    grad_short = result[5].transpose(1, 0, 2, 3).reshape(3, width, -1)
    return (merge(result[0]), merge(result[1]), merge(result[2]), merge(result[3]), grad_med, grad_short)
```

```python
import functools

import numpy as np
import jax
import jax.numpy as jnp
from jax import lax
from jax.experimental import pallas as pl
from jax.experimental.pallas import tpu as pltpu
from jax.sharding import PartitionSpec as P

HALO = 8
BF = jnp.bfloat16
F32 = jnp.float32


def split_np(x):
    hi = x.astype(np.float32).astype(BF)
    lo = (x - hi.astype(np.float64)).astype(np.float32).astype(BF)
    return hi, lo


def tables(length):
    size = 2 * length
    theta = np.pi * (2 * np.arange(length) + 1)[:, None] / size

    def forward(places):
        angle = theta * places[None, :]
        hi, lo = split_np(np.concatenate([np.cos(angle), -np.sin(angle)], axis=0))
        return np.concatenate([hi, lo], axis=1)

    def inverse(places):
        angle = theta * places[None, :]
        both = np.concatenate([np.cos(angle), -np.sin(angle)], axis=0).T * (2.0 / size)
        hi, lo = split_np(both)
        return np.concatenate([hi, lo], axis=0)

    n = np.arange(length)
    return np.stack([forward(n), forward(n + length), inverse(n + length), inverse(n), inverse(n - length)])


def dot(a, b):
    return jnp.dot(a, b, preferred_element_type=F32)


def short_conv(pad_ref, taps, width, count):
    total = taps[0:1] * pad_ref[pl.ds(HALO, count)]
    for j in range(1, width):
        total = total + taps[j : j + 1] * pad_ref[pl.ds(HALO - j, count)]
    return total


def first_kernel(width, q_ref, k_ref, v_ref, g_ref, halo_ref, s_ref, u_ref, d_ref, pad_ref):
    count = q_ref.shape[0]

    def conv(i, ref):
        pad_ref[0:HALO] = halo_ref[i].astype(F32)
        pad_ref[HALO:] = ref[...].astype(F32)
        return short_conv(pad_ref, s_ref[i], width, count)

    ks = conv(1, k_ref)
    u_ref[...] = (ks * conv(2, v_ref)).astype(BF)
    d_ref[...] = (g_ref[...].astype(F32) * conv(0, q_ref)).astype(BF)


def second_kernel(width, *refs):
    q_ref, k_ref, v_ref, g_ref, halo_ref, s_ref, uo_ref, up_ref, do_ref, dn_ref, h_ref, tab_ref = refs[:12]
    mixed_ref, gq_ref, gk_ref, gv_ref, acc_ref, head_ref, tail_ref = refs[-11:-4]
    padq, padk, padv, padg = refs[-4:]
    length = q_ref.shape[0]
    chans = q_ref.shape[1]

    def double(x):
        return jnp.concatenate([x, x], axis=0)

    wave = dot(tab_ref[0], double(up_ref[...])) + dot(tab_ref[1], double(uo_ref[...]))
    own = dot(tab_ref[0], double(do_ref[...]))
    ahead = own + dot(tab_ref[1], double(dn_ref[...]))
    filt = dot(tab_ref[0], double(h_ref[...].reshape(length, chans)))

    def times(a, b, sign):
        ar, ai = a[:length], a[length:]
        br, bi = b[:length], b[length:]
        if sign > 0:
            return jnp.concatenate([ar * br - ai * bi, ar * bi + ai * br], axis=0)
        return jnp.concatenate([ar * br + ai * bi, ai * br - ar * bi], axis=0)

    def back(spectrum, index):
        hi = spectrum.astype(BF)
        lo = (spectrum - hi.astype(F32)).astype(BF)
        both = dot(tab_ref[index], hi)
        return both[:length] + both[length:] + dot(tab_ref[index, :length], lo)

    z = back(times(wave, filt, 1), 2)
    du = back(times(ahead, filt, -1), 3)
    gm = back(times(own, wave, -1), 4)

    parts = acc_ref.shape[0]
    share = length // parts
    acc_ref[:, 0, :share] = gm.reshape(parts, share, chans)
    acc_ref[:, 0, share:] = jnp.zeros((parts, acc_ref.shape[2] - share, chans), F32)

    def load(i, ref, pad):
        pad[0:HALO] = halo_ref[i].astype(F32)
        pad[HALO:] = ref[...].astype(F32)
        return short_conv(pad, s_ref[i], width, length)

    padg[0:HALO] = jnp.zeros((HALO, chans), F32)
    padg[HALO + length :] = jnp.zeros((HALO, chans), F32)

    def finish(i, grads, pad, out_ref):
        padg[HALO : HALO + length] = grads
        taps = s_ref[i]
        total = taps[0:1] * grads
        head = taps[1:2] * padg[1 : 1 + HALO]
        sums = [jnp.sum(grads * pad[HALO : HALO + length], axis=0, keepdims=True)]
        for j in range(1, width):
            total = total + taps[j : j + 1] * padg[pl.ds(HALO + j, length)]
            if j > 1:
                head = head + taps[j : j + 1] * padg[j : j + HALO]
            sums.append(jnp.sum(grads * pad[pl.ds(HALO - j, length)], axis=0, keepdims=True))
        out_ref[...] = total.astype(BF)
        head_ref[i] = head.astype(BF)
        tail_ref[i] = total[length - HALO :]
        slot = acc_ref.shape[2] - share
        row = i * HALO
        acc_ref[row // slot, 0, pl.ds(share + row % slot, width)] = jnp.concatenate(sums, axis=0)

    qs = load(0, q_ref, padq)
    mixed_ref[...] = (qs * z).astype(BF)
    finish(0, g_ref[...].astype(F32) * z, padq, gq_ref)
    ks = load(1, k_ref, padk)
    vs = load(2, v_ref, padv)
    finish(1, du * vs, padk, gk_ref)
    finish(2, du * ks, padv, gv_ref)


def per_device(n_dp, n_ctx, query_in, key_in, value_in, grad_out, med_filter, short_filter):
    q, k, v, g = (a[0] for a in (query_in, key_in, value_in, grad_out))
    length, full = q.shape
    width = short_filter.shape[2]
    chans = full // n_ctx
    share = med_filter.shape[1]
    pieces = max(1, min(4, chans // 128))
    part = chans // pieces
    cb = 256 if part % 256 == 0 else 128
    inner = part // cb
    slot = HALO * (-(-3 // n_dp))
    right = [(i, i + 1) for i in range(n_ctx - 1)]
    left = [(i + 1, i) for i in range(n_ctx - 1)]
    assert n_dp * share == length and width - 1 <= HALO

    shorts = jnp.pad(short_filter.transpose(0, 2, 1), ((0, 0), (0, HALO - width), (0, 0)))
    shorts = lax.all_gather(shorts, "context")
    taps = lax.all_gather(med_filter.astype(BF).T, "context")
    taps = lax.all_gather(taps, "dp")
    table = jnp.asarray(tables(length))

    rim = jnp.stack([a[length - HALO :] for a in (q, k, v)])
    rim = rim.reshape(3, HALO, n_ctx, pieces, part)
    rims = [lax.ppermute(rim[:, :, :, c].reshape(3, HALO, n_ctx * part), "context", right) for c in range(pieces)]

    def whole(c):
        return pl.BlockSpec((length, cb), lambda b, i: (0, b * (chans // cb) + c * inner + i))

    piece = pl.BlockSpec((length, cb), lambda b, i: (0, b * inner + i))
    rim_spec = pl.BlockSpec((3, HALO, cb), lambda b, i: (0, 0, b * inner + i))

    def short_spec(c):
        return pl.BlockSpec((pl.squeezed, 3, HALO, cb), lambda b, i: (b, 0, 0, c * inner + i))

    sent = []
    for c in range(pieces):
        sent.append(
            pl.pallas_call(
                functools.partial(first_kernel, width),
                grid=(n_ctx, inner),
                in_specs=[whole(c)] * 4 + [rim_spec, short_spec(c)],
                out_specs=[piece] * 2,
                out_shape=[jax.ShapeDtypeStruct((length, n_ctx * part), BF)] * 2,
                scratch_shapes=[pltpu.VMEM((HALO + length, cb), F32)],
                cost_estimate=pl.CostEstimate(
                    flops=50 * length * n_ctx * part, bytes_accessed=24 * length * n_ctx * part, transcendentals=0
                ),
                name="featurize",
            )(q, k, v, g, rims[c], shorts)
        )
    arrived = [
        (lax.ppermute(u, "context", right), lax.ppermute(d, "context", left)) for u, d in sent
    ]

    grown = None
    sums = []
    heads = []
    tails = []
    for c in range(pieces):
        tap_spec = pl.BlockSpec((n_dp, 1, share, cb), lambda b, i, c=c: (0, b, 0, c * inner + i))
        table_spec = pl.BlockSpec(table.shape, lambda b, i: (0, 0, 0))
        args = [q, k, v, g, rims[c], shorts, sent[c][0], arrived[c][0], sent[c][1], arrived[c][1], taps, table]
        specs = [whole(c)] * 4 + [rim_spec, short_spec(c)] + [piece] * 4 + [tap_spec, table_spec]
        alias = {}
        if grown is not None:
            alias = {len(args) + i: i for i in range(4)}
            args += grown
            specs += [pl.BlockSpec(memory_space=pl.ANY)] * 4
        outs = pl.pallas_call(
            functools.partial(second_kernel, width),
            grid=(n_ctx, inner),
            in_specs=specs,
            out_specs=[whole(c)] * 4
            + [pl.BlockSpec((n_dp, 1, share + slot, cb), lambda b, i: (0, b, 0, i)), rim_spec, rim_spec],
            out_shape=[jax.ShapeDtypeStruct((length, full), BF)] * 4
            + [
                jax.ShapeDtypeStruct((n_dp, n_ctx, share + slot, part), F32),
                jax.ShapeDtypeStruct((3, HALO, n_ctx * part), BF),
                jax.ShapeDtypeStruct((3, HALO, n_ctx * part), F32),
            ],
            scratch_shapes=[pltpu.VMEM((HALO + length, cb), F32)] * 3 + [pltpu.VMEM((2 * HALO + length, cb), F32)],
            input_output_aliases=alias,
            cost_estimate=pl.CostEstimate(
                flops=4000 * length * n_ctx * part, bytes_accessed=80 * length * n_ctx * part, transcendentals=0
            ),
            compiler_params=pltpu.CompilerParams(vmem_limit_bytes=48 * 1024 * 1024),
            name="mixer",
        )(*args)
        grown = list(outs[:4])
        total = lax.psum_scatter(outs[4], "dp", scatter_dimension=0)
        sums.append(lax.psum_scatter(total, "context", scatter_dimension=0))
        heads.append(lax.ppermute(outs[5], "context", left))
        tails.append(outs[6])

    def join(items):
        return jnp.concatenate([a.reshape(3, HALO, n_ctx, 1, part) for a in items], axis=3).reshape(3, HALO, full)

    fixed = (join(tails) + join(heads).astype(F32)).astype(BF)
    grads = [lax.dynamic_update_slice(a, fixed[i], (length - HALO, 0)) for i, a in enumerate(grown[1:])]
    total = jnp.concatenate(sums, axis=1)
    grad_med = total[:share].T
    short = lax.all_gather(total[share:], "dp", tiled=True)[: 3 * HALO]
    grad_short = short.reshape(3, HALO, chans)[:, :width].transpose(0, 2, 1)
    return (grown[0][None], grads[0][None], grads[1][None], grads[2][None], grad_med, grad_short)


def solution(mesh):
    rows = P("dp", "context", None)
    med = P("context", "dp")
    short = P(None, "context", None)
    return jax.shard_map(
        functools.partial(per_device, mesh.shape["dp"], mesh.shape["context"]),
        mesh=mesh,
        in_specs=(rows, rows, rows, rows, med, short),
        out_specs=(rows, rows, rows, rows, med, short),
        check_vma=False,
    )
```

```python
import functools

import numpy as np
import jax
import jax.numpy as jnp
from jax import lax
from jax.experimental import pallas as pl
from jax.experimental.pallas import tpu as pltpu
from jax.sharding import PartitionSpec as P

HALO = 8
BF = jnp.bfloat16
F32 = jnp.float32


def split_np(x):
    hi = x.astype(np.float32).astype(BF)
    lo = (x - hi.astype(np.float64)).astype(np.float32).astype(BF)
    return hi, lo


def tables(length):
    size = 2 * length
    theta = np.pi * (2 * np.arange(length) + 1)[:, None] / size

    def forward(places):
        angle = theta * places[None, :]
        hi, lo = split_np(np.concatenate([np.cos(angle), -np.sin(angle)], axis=0))
        return np.concatenate([hi, lo], axis=1)

    def inverse(places):
        angle = theta * places[None, :]
        both = np.concatenate([np.cos(angle), -np.sin(angle)], axis=0).T * (2.0 / size)
        hi, lo = split_np(both)
        return np.concatenate([hi, lo], axis=0)

    n = np.arange(length)
    return np.stack([forward(n), forward(n + length), inverse(n + length), inverse(n), inverse(n - length)])


def dot(a, b):
    return jnp.dot(a, b, preferred_element_type=F32)


def short_conv(pad_ref, taps, width, count):
    total = taps[0:1] * pad_ref[pl.ds(HALO, count)]
    for j in range(1, width):
        total = total + taps[j : j + 1] * pad_ref[pl.ds(HALO - j, count)]
    return total


def bits_of(count):
    return [b for b in range(count.bit_length() - 1)]


def swap(x, axis, count, bit):
    return lax.ppermute(x, axis, [(i, i ^ (1 << bit)) for i in range(count)])


def gather(block, axis, count):
    me = lax.axis_index(axis)
    rest = block.shape
    zeros = (0,) * len(rest)
    held = lax.dynamic_update_slice(jnp.zeros((count,) + rest, block.dtype), block[None], (me,) + zeros)
    for bit in reversed(bits_of(count)):
        low = 1 << bit
        view = held.reshape((count // (2 * low), 2, low) + rest)
        mine = (me // low) % 2
        own = lax.dynamic_slice(view, (0, mine, me % low) + zeros, (count // (2 * low), 1, 1) + rest)
        other = swap(own, axis, count, bit)
        view = lax.dynamic_update_slice(view, other, (0, 1 - mine, me % low) + zeros)
        held = view.reshape((count,) + rest)
    return held


def scatter_sum(x, axis, count, narrow):
    me = lax.axis_index(axis)
    for bit in bits_of(count):
        mine = (me >> bit) % 2
        view = x.reshape((x.shape[0] // 2, 2) + x.shape[1:])
        send = lax.dynamic_index_in_dim(view, 1 - mine, 1, keepdims=False)
        keep = lax.dynamic_index_in_dim(view, mine, 1, keepdims=False)
        if bit in narrow:
            send = send.astype(BF)
        x = keep + swap(send, axis, count, bit).astype(F32)
    return x[0]


def first_kernel(width, q_ref, k_ref, v_ref, g_ref, halo_ref, s_ref, u_ref, d_ref, pad_ref):
    count = q_ref.shape[0]

    def conv(i, ref):
        pad_ref[0:HALO] = halo_ref[i].astype(F32)
        pad_ref[HALO:] = ref[...].astype(F32)
        return short_conv(pad_ref, s_ref[i // s_ref.shape[1], i % s_ref.shape[1]], width, count)

    ks = conv(1, k_ref)
    u_ref[...] = (ks * conv(2, v_ref)).astype(BF)
    d_ref[...] = (g_ref[...].astype(F32) * conv(0, q_ref)).astype(BF)


def second_kernel(width, *refs):
    q_ref, k_ref, v_ref, g_ref, halo_ref, s_ref, uo_ref, up_ref, do_ref, dn_ref, h_ref, tab_ref = refs[:12]
    mixed_ref, gq_ref, gk_ref, gv_ref, acc_ref, head_ref, tail_ref = refs[-11:-4]
    padq, padk, padv, padg = refs[-4:]
    length = q_ref.shape[0]
    chans = q_ref.shape[1]

    def taps_of(i):
        return s_ref[i // s_ref.shape[1], i % s_ref.shape[1]]

    def double(x):
        return jnp.concatenate([x, x], axis=0)

    wave = dot(tab_ref[0], double(up_ref[...])) + dot(tab_ref[1], double(uo_ref[...]))
    own = dot(tab_ref[0], double(do_ref[...]))
    ahead = own + dot(tab_ref[1], double(dn_ref[...]))
    filt = dot(tab_ref[0], double(h_ref[...].reshape(length, chans)))

    def times(a, b, sign):
        ar, ai = a[:length], a[length:]
        br, bi = b[:length], b[length:]
        if sign > 0:
            return jnp.concatenate([ar * br - ai * bi, ar * bi + ai * br], axis=0)
        return jnp.concatenate([ar * br + ai * bi, ai * br - ar * bi], axis=0)

    def back(spectrum, index):
        hi = spectrum.astype(BF)
        lo = (spectrum - hi.astype(F32)).astype(BF)
        both = dot(tab_ref[index], hi)
        return both[:length] + both[length:] + dot(tab_ref[index, :length], lo)

    z = back(times(wave, filt, 1), 2)
    du = back(times(ahead, filt, -1), 3)
    gm = back(times(own, wave, -1), 4)

    parts = acc_ref.shape[0]
    share = length // parts
    acc_ref[:, 0, :share] = gm.reshape(parts, share, chans)
    acc_ref[:, 0, share:] = jnp.zeros((parts, acc_ref.shape[2] - share, chans), F32)

    def load(i, ref, pad):
        pad[0:HALO] = halo_ref[i].astype(F32)
        pad[HALO:] = ref[...].astype(F32)
        return short_conv(pad, taps_of(i), width, length)

    padg[0:HALO] = jnp.zeros((HALO, chans), F32)
    padg[HALO + length :] = jnp.zeros((HALO, chans), F32)

    def finish(i, grads, pad, out_ref):
        padg[HALO : HALO + length] = grads
        taps = taps_of(i)
        total = taps[0:1] * grads
        head = taps[1:2] * padg[1 : 1 + HALO]
        sums = [jnp.sum(grads * pad[HALO : HALO + length], axis=0, keepdims=True)]
        for j in range(1, width):
            total = total + taps[j : j + 1] * padg[pl.ds(HALO + j, length)]
            if j > 1:
                head = head + taps[j : j + 1] * padg[j : j + HALO]
            sums.append(jnp.sum(grads * pad[pl.ds(HALO - j, length)], axis=0, keepdims=True))
        out_ref[...] = total.astype(BF)
        head_ref[i] = head.astype(BF)
        tail_ref[i] = total[length - HALO :]
        slot = acc_ref.shape[2] - share
        row = i * HALO
        acc_ref[row // slot, 0, pl.ds(share + row % slot, width)] = jnp.concatenate(sums, axis=0)

    qs = load(0, q_ref, padq)
    mixed_ref[...] = (qs * z).astype(BF)
    finish(0, g_ref[...].astype(F32) * z, padq, gq_ref)
    ks = load(1, k_ref, padk)
    vs = load(2, v_ref, padv)
    finish(1, du * vs, padk, gk_ref)
    finish(2, du * ks, padv, gv_ref)


def per_device(n_dp, n_ctx, query_in, key_in, value_in, grad_out, med_filter, short_filter):
    q, k, v, g = (a[0] for a in (query_in, key_in, value_in, grad_out))
    length, full = q.shape
    width = short_filter.shape[2]
    chans = full // n_ctx
    share = med_filter.shape[1]
    pieces = max(1, min(4, chans // 128))
    part = chans // pieces
    cb = 256 if part % 256 == 0 else 128
    inner = part // cb
    per = -(-3 // n_dp)
    slot = HALO * per
    right = [(i, i + 1) for i in range(n_ctx - 1)]
    left = [(i + 1, i) for i in range(n_ctx - 1)]
    assert n_dp * share == length and width - 1 <= HALO

    shorts = jnp.pad(short_filter.transpose(0, 2, 1), ((0, n_dp * per - 3), (0, HALO - width), (0, 0)))
    shorts = lax.dynamic_slice_in_dim(shorts, lax.axis_index("dp") * per, per, 0)
    shorts = gather(gather(shorts, "context", n_ctx), "dp", n_dp)
    taps, shorts = lax.optimization_barrier((med_filter.astype(BF).T, shorts))
    taps = gather(gather(taps, "context", n_ctx), "dp", n_dp)
    table = jnp.asarray(tables(length))

    rim = jnp.stack([a[length - HALO :] for a in (q, k, v)])
    rims = lax.ppermute(rim, "context", right)

    def whole(c):
        return pl.BlockSpec((length, cb), lambda b, i: (0, b * (chans // cb) + c * inner + i))

    piece = pl.BlockSpec((length, cb), lambda b, i: (0, b * inner + i))
    rim_spec = pl.BlockSpec((3, HALO, cb), lambda b, i: (0, 0, b * inner + i))

    def edge(c):
        return pl.BlockSpec((3, HALO, cb), lambda b, i: (0, 0, b * (chans // cb) + c * inner + i))

    def short_spec(c):
        return pl.BlockSpec((n_dp, pl.squeezed, per, HALO, cb), lambda b, i: (0, b, 0, 0, c * inner + i))

    sent = []
    for c in range(pieces):
        sent.append(
            pl.pallas_call(
                functools.partial(first_kernel, width),
                grid=(n_ctx, inner),
                in_specs=[whole(c)] * 4 + [edge(c), short_spec(c)],
                out_specs=[piece] * 2,
                out_shape=[jax.ShapeDtypeStruct((length, n_ctx * part), BF)] * 2,
                scratch_shapes=[pltpu.VMEM((HALO + length, cb), F32)],
                cost_estimate=pl.CostEstimate(
                    flops=50 * length * n_ctx * part, bytes_accessed=24 * length * n_ctx * part, transcendentals=0
                ),
                name="featurize",
            )(q, k, v, g, rims, shorts)
        )
    arrived = [
        (lax.ppermute(u, "context", right), lax.ppermute(d, "context", left)) for u, d in sent
    ]

    grown = None
    sums = []
    heads = []
    tails = []
    for c in range(pieces):
        tap_spec = pl.BlockSpec((n_dp, 1, share, cb), lambda b, i, c=c: (0, b, 0, c * inner + i))
        table_spec = pl.BlockSpec(table.shape, lambda b, i: (0, 0, 0))
        args = [q, k, v, g, rims, shorts, sent[c][0], arrived[c][0], sent[c][1], arrived[c][1], taps, table]
        specs = [whole(c)] * 4 + [edge(c), short_spec(c)] + [piece] * 4 + [tap_spec, table_spec]
        alias = {}
        if grown is not None:
            alias = {len(args) + i: i for i in range(4)}
            args += grown
            specs += [pl.BlockSpec(memory_space=pl.ANY)] * 4
        outs = pl.pallas_call(
            functools.partial(second_kernel, width),
            grid=(n_ctx, inner),
            in_specs=specs,
            out_specs=[whole(c)] * 4
            + [pl.BlockSpec((n_dp, 1, share + slot, cb), lambda b, i: (0, b, 0, i)), rim_spec, rim_spec],
            out_shape=[jax.ShapeDtypeStruct((length, full), BF)] * 4
            + [
                jax.ShapeDtypeStruct((n_dp, n_ctx, share + slot, part), F32),
                jax.ShapeDtypeStruct((3, HALO, n_ctx * part), BF),
                jax.ShapeDtypeStruct((3, HALO, n_ctx * part), F32),
            ],
            scratch_shapes=[pltpu.VMEM((HALO + length, cb), F32)] * 3 + [pltpu.VMEM((2 * HALO + length, cb), F32)],
            input_output_aliases=alias,
            cost_estimate=pl.CostEstimate(
                flops=4000 * length * n_ctx * part, bytes_accessed=80 * length * n_ctx * part, transcendentals=0
            ),
            compiler_params=pltpu.CompilerParams(vmem_limit_bytes=48 * 1024 * 1024),
            name="mixer",
        )(*args)
        grown = list(outs[:4])
        sums.append(outs[4])
        heads.append(outs[5])
        tails.append(outs[6])

    def reduce(items):
        x = jnp.concatenate(items, axis=3) if len(items) > 1 else items[0]
        x = scatter_sum(x, "dp", n_dp, (1,))
        return scatter_sum(x, "context", n_ctx, (0,))

    groups = [(0, pieces - 1), (pieces - 1, pieces)] if pieces > 1 else [(0, 1)]
    sums = [reduce(sums[a:b]) for a, b in groups]
    heads = [
        h for a, b in groups for h in jnp.split(lax.ppermute(jnp.concatenate(heads[a:b], axis=0), "context", left), b - a)
    ]

    def join(items):
        return jnp.concatenate([a.reshape(3, HALO, n_ctx, 1, part) for a in items], axis=3).reshape(3, HALO, full)

    fixed = (join(tails) + join(heads).astype(F32)).astype(BF)
    grads = [lax.dynamic_update_slice(a, fixed[i], (length - HALO, 0)) for i, a in enumerate(grown[1:])]
    total = jnp.concatenate(sums, axis=1)
    grad_med = total[:share].T
    short = gather(total[share:], "dp", n_dp).reshape(-1, chans)[: 3 * HALO]
    grad_short = short.reshape(3, HALO, chans)[:, :width].transpose(0, 2, 1)
    return (grown[0][None], grads[0][None], grads[1][None], grads[2][None], grad_med, grad_short)


def solution(mesh):
    rows = P("dp", "context", None)
    med = P("context", "dp")
    short = P(None, "context", None)
    return jax.shard_map(
        functools.partial(per_device, mesh.shape["dp"], mesh.shape["context"]),
        mesh=mesh,
        in_specs=(rows, rows, rows, rows, med, short),
        out_specs=(rows, rows, rows, rows, med, short),
        check_vma=False,
    )
```

```python
import functools

import numpy as np
import jax
import jax.numpy as jnp
from jax import lax
from jax.experimental import pallas as pl
from jax.experimental.pallas import tpu as pltpu
from jax.sharding import PartitionSpec as P

HALO = 8
BF = jnp.bfloat16
F32 = jnp.float32


def split_np(x):
    hi = x.astype(np.float32).astype(BF)
    lo = (x - hi.astype(np.float64)).astype(np.float32).astype(BF)
    return hi, lo


def tables(length):
    size = 2 * length
    theta = np.pi * (2 * np.arange(length) + 1)[:, None] / size

    def forward(places):
        angle = theta * places[None, :]
        hi, lo = split_np(np.concatenate([np.cos(angle), -np.sin(angle)], axis=0))
        return np.concatenate([hi, lo], axis=1)

    def inverse(places):
        angle = theta * places[None, :]
        both = np.concatenate([np.cos(angle), -np.sin(angle)], axis=0).T * (2.0 / size)
        hi, lo = split_np(both)
        return np.concatenate([hi, lo], axis=0)

    n = np.arange(length)
    return np.stack([forward(n), forward(n + length), inverse(n + length), inverse(n), inverse(n - length)])


def dot(a, b):
    return jnp.dot(a, b, preferred_element_type=F32)


def short_conv(pad_ref, taps, width, count):
    total = taps[0:1] * pad_ref[pl.ds(HALO, count)]
    for j in range(1, width):
        total = total + taps[j : j + 1] * pad_ref[pl.ds(HALO - j, count)]
    return total


def bits_of(count):
    return [b for b in range(count.bit_length() - 1)]


def swap(x, axis, count, bit):
    return lax.ppermute(x, axis, [(i, i ^ (1 << bit)) for i in range(count)])


def gather(block, axis, count, after=()):
    after = list(after)
    me = lax.axis_index(axis)
    rest = block.shape
    zeros = (0,) * len(rest)
    held = lax.dynamic_update_slice(jnp.zeros((count,) + rest, block.dtype), block[None], (me,) + zeros)
    for bit in reversed(bits_of(count)):
        low = 1 << bit
        view = held.reshape((count // (2 * low), 2, low) + rest)
        mine = (me // low) % 2
        own = lax.dynamic_slice(view, (0, mine, me % low) + zeros, (count // (2 * low), 1, 1) + rest)
        if after:
            own, _ = lax.optimization_barrier((own, after.pop(0)))
        other = swap(own, axis, count, bit)
        view = lax.dynamic_update_slice(view, other, (0, 1 - mine, me % low) + zeros)
        held = view.reshape((count,) + rest)
    return held


def scatter_sum(x, axis, count, narrow):
    me = lax.axis_index(axis)
    for bit in bits_of(count):
        mine = (me >> bit) % 2
        view = x.reshape((x.shape[0] // 2, 2) + x.shape[1:])
        send = lax.dynamic_index_in_dim(view, 1 - mine, 1, keepdims=False)
        keep = lax.dynamic_index_in_dim(view, mine, 1, keepdims=False)
        if bit in narrow:
            send = send.astype(BF)
        x = keep + swap(send, axis, count, bit).astype(F32)
    return x[0]


def first_kernel(width, q_ref, k_ref, v_ref, g_ref, halo_ref, s_ref, u_ref, d_ref, pad_ref):
    count = q_ref.shape[0]

    def conv(i, ref):
        pad_ref[0:HALO] = halo_ref[i].astype(F32)
        pad_ref[HALO:] = ref[...].astype(F32)
        return short_conv(pad_ref, s_ref[i // s_ref.shape[1], i % s_ref.shape[1]], width, count)

    ks = conv(1, k_ref)
    u_ref[...] = (ks * conv(2, v_ref)).astype(BF)
    d_ref[...] = (g_ref[...].astype(F32) * conv(0, q_ref)).astype(BF)


def second_kernel(width, *refs):
    q_ref, k_ref, v_ref, g_ref, halo_ref, s_ref, uo_ref, up_ref, do_ref, dn_ref, h_ref, tab_ref = refs[:12]
    mixed_ref, gq_ref, gk_ref, gv_ref, acc_ref, head_ref, tail_ref = refs[-11:-4]
    padq, padk, padv, padg = refs[-4:]
    length = q_ref.shape[0]
    chans = q_ref.shape[1]

    def taps_of(i):
        return s_ref[i // s_ref.shape[1], i % s_ref.shape[1]]

    def double(x):
        return jnp.concatenate([x, x], axis=0)

    wave = dot(tab_ref[0], double(up_ref[...])) + dot(tab_ref[1], double(uo_ref[...]))
    own = dot(tab_ref[0], double(do_ref[...]))
    ahead = own + dot(tab_ref[1], double(dn_ref[...]))
    filt = dot(tab_ref[0], double(h_ref[...].reshape(length, chans)))

    def times(a, b, sign):
        ar, ai = a[:length], a[length:]
        br, bi = b[:length], b[length:]
        if sign > 0:
            return jnp.concatenate([ar * br - ai * bi, ar * bi + ai * br], axis=0)
        return jnp.concatenate([ar * br + ai * bi, ai * br - ar * bi], axis=0)

    def back(spectrum, index):
        hi = spectrum.astype(BF)
        lo = (spectrum - hi.astype(F32)).astype(BF)
        both = dot(tab_ref[index], hi)
        return both[:length] + both[length:] + dot(tab_ref[index, :length], lo)

    z = back(times(wave, filt, 1), 2)
    du = back(times(ahead, filt, -1), 3)
    gm = back(times(own, wave, -1), 4)

    parts = acc_ref.shape[0]
    share = length // parts
    acc_ref[:, 0, :share] = gm.reshape(parts, share, chans)
    acc_ref[:, 0, share:] = jnp.zeros((parts, acc_ref.shape[2] - share, chans), F32)

    def load(i, ref, pad):
        pad[0:HALO] = halo_ref[i].astype(F32)
        pad[HALO:] = ref[...].astype(F32)
        return short_conv(pad, taps_of(i), width, length)

    padg[0:HALO] = jnp.zeros((HALO, chans), F32)
    padg[HALO + length :] = jnp.zeros((HALO, chans), F32)

    def finish(i, grads, pad, out_ref):
        padg[HALO : HALO + length] = grads
        taps = taps_of(i)
        total = taps[0:1] * grads
        head = taps[1:2] * padg[1 : 1 + HALO]
        sums = [jnp.sum(grads * pad[HALO : HALO + length], axis=0, keepdims=True)]
        for j in range(1, width):
            total = total + taps[j : j + 1] * padg[pl.ds(HALO + j, length)]
            if j > 1:
                head = head + taps[j : j + 1] * padg[j : j + HALO]
            sums.append(jnp.sum(grads * pad[pl.ds(HALO - j, length)], axis=0, keepdims=True))
        out_ref[...] = total.astype(BF)
        head_ref[i] = head.astype(BF)
        tail_ref[i] = total[length - HALO :]
        slot = acc_ref.shape[2] - share
        row = i * HALO
        acc_ref[row // slot, 0, pl.ds(share + row % slot, width)] = jnp.concatenate(sums, axis=0)

    qs = load(0, q_ref, padq)
    mixed_ref[...] = (qs * z).astype(BF)
    finish(0, g_ref[...].astype(F32) * z, padq, gq_ref)
    ks = load(1, k_ref, padk)
    vs = load(2, v_ref, padv)
    finish(1, du * vs, padk, gk_ref)
    finish(2, du * ks, padv, gv_ref)


def per_device(n_dp, n_ctx, query_in, key_in, value_in, grad_out, med_filter, short_filter):
    q, k, v, g = (a[0] for a in (query_in, key_in, value_in, grad_out))
    length, full = q.shape
    width = short_filter.shape[2]
    chans = full // n_ctx
    share = med_filter.shape[1]
    pieces = max(1, min(2, chans // 128))
    part = chans // pieces
    cb = 512 if part % 512 == 0 else 128
    inner = part // cb
    per = -(-3 // n_dp)
    slot = HALO * per
    right = [(i, i + 1) for i in range(n_ctx - 1)]
    left = [(i + 1, i) for i in range(n_ctx - 1)]
    assert n_dp * share == length and width - 1 <= HALO

    shorts = jnp.pad(short_filter.transpose(0, 2, 1), ((0, n_dp * per - 3), (0, HALO - width), (0, 0)))
    shorts = lax.dynamic_slice_in_dim(shorts, lax.axis_index("dp") * per, per, 0)
    shorts = gather(gather(shorts, "context", n_ctx), "dp", n_dp)
    table = jnp.asarray(tables(length))

    rim = jnp.stack([a[length - HALO :] for a in (q, k, v)])
    rims = lax.ppermute(rim, "context", right)

    def whole(c):
        return pl.BlockSpec((length, cb), lambda b, i: (0, b * (chans // cb) + c * inner + i))

    piece = pl.BlockSpec((length, cb), lambda b, i: (0, b * inner + i))
    rim_spec = pl.BlockSpec((3, HALO, cb), lambda b, i: (0, 0, b * inner + i))

    def edge(c):
        return pl.BlockSpec((3, HALO, cb), lambda b, i: (0, 0, b * (chans // cb) + c * inner + i))

    def short_spec(c):
        return pl.BlockSpec((n_dp, pl.squeezed, per, HALO, cb), lambda b, i: (0, b, 0, 0, c * inner + i))

    sent = []
    for c in range(pieces):
        sent.append(
            pl.pallas_call(
                functools.partial(first_kernel, width),
                grid=(n_ctx, inner),
                in_specs=[whole(c)] * 4 + [edge(c), short_spec(c)],
                out_specs=[piece] * 2,
                out_shape=[jax.ShapeDtypeStruct((length, n_ctx * part), BF)] * 2,
                scratch_shapes=[pltpu.VMEM((HALO + length, cb), F32)],
                cost_estimate=pl.CostEstimate(
                    flops=50 * length * n_ctx * part, bytes_accessed=24 * length * n_ctx * part, transcendentals=0
                ),
                name="featurize",
            )(q, k, v, g, rims, shorts)
        )
    done = [u for u, _ in sent]
    taps = gather(med_filter.astype(BF).T, "context", n_ctx)
    taps = gather(taps, "dp", n_dp, done[:1])
    arrived = [
        (lax.ppermute(u, "context", right), lax.ppermute(d, "context", left)) for u, d in sent
    ]

    grown = None
    sums = []
    heads = []
    tails = []
    for c in range(pieces):
        tap_spec = pl.BlockSpec((n_dp, 1, share, cb), lambda b, i, c=c: (0, b, 0, c * inner + i))
        table_spec = pl.BlockSpec(table.shape, lambda b, i: (0, 0, 0))
        args = [q, k, v, g, rims, shorts, sent[c][0], arrived[c][0], sent[c][1], arrived[c][1], taps, table]
        specs = [whole(c)] * 4 + [edge(c), short_spec(c)] + [piece] * 4 + [tap_spec, table_spec]
        alias = {}
        if c == 0:
            args.append(done[-1])
            specs.append(pl.BlockSpec(memory_space=pl.ANY))
        if grown is not None:
            alias = {len(args) + i: i for i in range(4)}
            args += grown
            specs += [pl.BlockSpec(memory_space=pl.ANY)] * 4
        outs = pl.pallas_call(
            functools.partial(second_kernel, width),
            grid=(n_ctx, inner),
            in_specs=specs,
            out_specs=[whole(c)] * 4
            + [pl.BlockSpec((n_dp, 1, share + slot, cb), lambda b, i: (0, b, 0, i)), rim_spec, rim_spec],
            out_shape=[jax.ShapeDtypeStruct((length, full), BF)] * 4
            + [
                jax.ShapeDtypeStruct((n_dp, n_ctx, share + slot, part), F32),
                jax.ShapeDtypeStruct((3, HALO, n_ctx * part), BF),
                jax.ShapeDtypeStruct((3, HALO, n_ctx * part), F32),
            ],
            scratch_shapes=[pltpu.VMEM((HALO + length, cb), F32)] * 3 + [pltpu.VMEM((2 * HALO + length, cb), F32)],
            input_output_aliases=alias,
            cost_estimate=pl.CostEstimate(
                flops=4000 * length * n_ctx * part, bytes_accessed=80 * length * n_ctx * part, transcendentals=0
            ),
            compiler_params=pltpu.CompilerParams(vmem_limit_bytes=48 * 1024 * 1024),
            name="mixer",
        )(*args)
        grown = list(outs[:4])
        sums.append(outs[4])
        heads.append(outs[5])
        tails.append(outs[6])

    def reduce(items):
        x = jnp.concatenate(items, axis=3) if len(items) > 1 else items[0]
        x = scatter_sum(x, "dp", n_dp, (1,))
        return scatter_sum(x, "context", n_ctx, bits_of(n_ctx))

    half = pieces // 2
    groups = [(0, half), (half, pieces)] if pieces > 1 else [(0, 1)]
    sums = [reduce(sums[a:b]) for a, b in groups]
    heads = [
        h for a, b in groups for h in jnp.split(lax.ppermute(jnp.concatenate(heads[a:b], axis=0), "context", left), b - a)
    ]

    def join(items):
        return jnp.concatenate([a.reshape(3, HALO, n_ctx, 1, part) for a in items], axis=3).reshape(3, HALO, full)

    fixed = (join(tails) + join(heads).astype(F32)).astype(BF)
    grads = [lax.dynamic_update_slice(a, fixed[i], (length - HALO, 0)) for i, a in enumerate(grown[1:])]
    total = jnp.concatenate(sums, axis=1)
    grad_med = total[:share].T
    short = gather(total[share:], "dp", n_dp).reshape(-1, chans)[: 3 * HALO]
    grad_short = short.reshape(3, HALO, chans)[:, :width].transpose(0, 2, 1)
    return (grown[0][None], grads[0][None], grads[1][None], grads[2][None], grad_med, grad_short)


def solution(mesh):
    rows = P("dp", "context", None)
    med = P("context", "dp")
    short = P(None, "context", None)
    return jax.shard_map(
        functools.partial(per_device, mesh.shape["dp"], mesh.shape["context"]),
        mesh=mesh,
        in_specs=(rows, rows, rows, rows, med, short),
        out_specs=(rows, rows, rows, rows, med, short),
        check_vma=False,
    )
```
